32 devices in a mesh: seq: 8 (over z, x), expert: 4 (over y, core).
Axes of the slice: x: 2, y: 2, z: 4, core: 2. Of those that a mesh axis runs over, the one named last changes fastest.
Arguments:
- query: bfloat16 [32, 8192], P('expert'), may hold values from -100 to 100
- cached_key_block: bfloat16 [32, 1024, 512], P('expert', 'seq'), may hold values from -5 to 5
- cached_value_block: bfloat16 [32, 1024, 512], P('expert', 'seq'), may hold values from -6 to 6
- fresh_token_key: bfloat16 [32, 512], P('expert'), may hold values from -6 to 6
- fresh_token_value: bfloat16 [32, 512], P('expert'), may hold values from -6 to 6
- lengths: int32 [32], P('expert'), may hold values from 2 to 1024, as said below
- residual_in: bfloat16 [32, 4096], P('expert'), may hold values from -6 to 6
- o_weight: bfloat16 [8192, 4096], P('seq'), may hold values from -0.0625 to 0.0625
- norm_gain: float32 [4096], replicated, may hold values from 0.1 to 1.9
- gate_logits: float32 [32, 8], replicated, may hold values from -6 to 6
- routes: int32 [32, 8], replicated, may hold values from 0 to 63, all different within a row; in each aligned block of 8 rows (0 to 7, 8 to 15, ...) at most 2 rows name the same one
- w_gate: bfloat16 [128, 4096, 768], P(('seq', 'expert')), may hold values from -0.09375 to 0.09375
- w_up: bfloat16 [128, 4096, 768], P(('seq', 'expert')), may hold values from -0.09375 to 0.09375
- w_down: bfloat16 [128, 768, 4096], P(('seq', 'expert')), may hold values from -0.15625 to 0.15625
Outputs:
- layer_out: bfloat16 [32, 4096], P('expert', 'seq')
The draws below stay inside these ranges and needn't reach their ends.
Inputs may be any that keep to these rules, and one draw needn't show every extreme that they name: `lengths`: the first row of every aligned block of 8 rows has length 1024. `routes`: each row names 8 different experts. In every aligned block of 8 rows no expert is named by more than 2 rows, a bound that some block reaches.
All inputs are finite; a program needn't handle non-finite values.
Results may differ from the reference program's by a relative error of at most 0.0044.
Values may be sent and summed in bfloat16 or wider, within the bound.
A program may use at most 192 MiB of HBM per device.

```python
import math
import jax
import jax.numpy as jnp
import numpy as np
from jax import lax

D = 4096
QUERY_HEADS = 64
KEY_VALUE_HEADS = 4
HEAD_SIZE = 128
FF = 1536
EXPERTS = 64
TOP = 8
CAP = 2
ROWS_GRP = 8
TOTAL_ROWS = 32
CACHE_LENGTH = 1024
N_EXPERT = 4


def cache_keys(key):
    return jax.random.truncated_normal(key, -4.0, 4.0, (TOTAL_ROWS, CACHE_LENGTH, KEY_VALUE_HEADS * HEAD_SIZE), jnp.float32)


def draw_cached_key_block(key, part):
    keys_base = cache_keys(key)
    return keys_base.astype(jnp.bfloat16)


def draw_query(key, part):
    key = jax.random.fold_in(key, 5)
    entries = jax.random.truncated_normal(key, -4.0, 4.0, (TOTAL_ROWS, QUERY_HEADS * HEAD_SIZE), jnp.float32)
    return entries.astype(jnp.bfloat16)


def draw_lengths(key, part):
    key = jax.random.fold_in(key, 7)
    drawn = jax.random.randint(key, (TOTAL_ROWS,), 2, CACHE_LENGTH + 1, dtype=jnp.int32)
    return jnp.where(jnp.arange(TOTAL_ROWS, dtype=jnp.int32) % ROWS_GRP == 0, CACHE_LENGTH, drawn).astype(jnp.int32)


def block_scale(rng, dims, pieces, low, top_value):
    def one(position, parts):
        heights = jax.random.uniform(jax.random.fold_in(jax.random.fold_in(rng, 6), position), (parts,), jnp.float32, low / len(pieces), top_value / len(pieces))
        return jnp.repeat(jnp.exp(heights), dims[position] // parts).reshape((-1,) + (1,) * (len(dims) - position - 1))

    loudness = one(*pieces[0])
    for cut in pieces[1:]:
        loudness = loudness * one(*cut)
    return loudness


def deal_out(own_key, own, number, rows, amount, top, bound, lean):
    ranking = jax.random.permutation(own_key, amount)
    packed, usual = portions_of(amount, rows * top, bound, lean, True), portions_of(amount, rows * top, bound, lean, False)
    places = jnp.arange(amount)

    def named(tallies, rotation):
        used = int((tallies > 0).sum())
        fixed = max(1, used // 4)
        moved = fixed + (places - fixed + rotation * (used - fixed)) % max(1, amount - fixed)
        return jnp.zeros((amount,), jnp.int32).at[ranking[jnp.where(places < fixed, places, moved)]].set(jnp.asarray(tallies, jnp.int32))

    tallies = jnp.where(number % 4 == 0, named(packed, number // 4), named(usual, number - number // 4 - 1))
    mixed = jax.random.permutation(jax.random.fold_in(own, 3), amount)
    giver, taker = mixed[0:amount // 2 * 2:2], mixed[1:amount // 2 * 2:2]
    margin = jnp.minimum(tallies[giver] - 1, bound - tallies[taker]) // 2
    margin = jnp.where((giver == ranking[0]) | (taker == ranking[0]) | (tallies[taker] == 0), 0, jnp.maximum(margin, 0))
    moved = jax.random.randint(jax.random.fold_in(own, 4), (amount // 2,), 0, 1 << 20) % (margin + 1)
    tallies = tallies.at[giver].add(-moved).at[taker].add(moved)
    members = jnp.searchsorted(jnp.cumsum(tallies), jnp.arange(rows * top), side="right").astype(jnp.int32)
    table = members.reshape(top, rows).T
    table = table[jax.random.permutation(jax.random.fold_in(own, 1), rows)]
    rotation = jax.random.randint(jax.random.fold_in(own, 2), (rows, 1), 0, top)
    return jnp.take_along_axis(table, (jnp.arange(top)[None, :] + rotation) % top, axis=1)


def portions_of(number_of, total, reach, skew, full):
    loads = [(1 << 20) // math.isqrt(rank ** skew) + 1 for rank in range(1, number_of + 1)]
    largest = reach if full else min(reach, max(-(-total // number_of), total * loads[0] // sum(loads)))
    least = 1 if total - largest >= number_of - 1 else 0
    counts, surplus = [largest] + [least] * (number_of - 1), total - largest - least * (number_of - 1)
    while surplus > 0:
        free = [i for i in range(1, number_of) if counts[i] < largest] or [i for i in range(1, number_of) if counts[i] < reach]
        mass, remaining = sum([loads[i] for i in free]), surplus
        for i in free:
            more = min(reach - counts[i], max(1, remaining * loads[i] // mass), surplus)
            counts[i] = counts[i] + more
            surplus = surplus - more
    return np.array(counts)


def gaussian(rng, dims, scale, reach, cuts=(), held_as=jnp.bfloat16):
    loudness = block_scale(rng, dims, cuts, -0.22, 0.18) if cuts else 1.0
    entries = jax.random.normal(rng, dims, jnp.float32) * scale * loudness
    return jnp.minimum(jnp.maximum(entries, -reach), reach).astype(held_as)


def setup_inputs(seed: int = 0) -> dict:
    keys = jax.random.split(jax.random.key(seed), 15)
    query = draw_query(jax.random.fold_in(keys[14], 71), 0)
    cached_key_block = draw_cached_key_block(jax.random.fold_in(keys[14], 71), 0)
    cached_value_block = gaussian(keys[2], (TOTAL_ROWS, CACHE_LENGTH, KEY_VALUE_HEADS * HEAD_SIZE), 1.0, 6.0, ((0, 4), (1, 8)))
    fresh_token_key = gaussian(keys[3], (TOTAL_ROWS, KEY_VALUE_HEADS * HEAD_SIZE), 1.0, 6.0, ((0, 4),))
    fresh_token_value = gaussian(keys[4], (TOTAL_ROWS, KEY_VALUE_HEADS * HEAD_SIZE), 1.0, 6.0, ((0, 4),))
    lengths = draw_lengths(jax.random.fold_in(keys[14], 71), 0)
    residual_in = gaussian(keys[6], (TOTAL_ROWS, D), 1.0, 6.0, ((0, 4),))
    o_weight = gaussian(keys[7], (QUERY_HEADS * HEAD_SIZE, D), (QUERY_HEADS * HEAD_SIZE) ** -0.5, 0.0625, ((0, 8),))
    norm_gain = jnp.clip(1.0 + 0.18 * jax.random.normal(keys[8], (D,), jnp.float32), 0.1, 1.9)
    gate_logits = gaussian(keys[9], (TOTAL_ROWS, TOP), 1.5, 6.0, (), jnp.float32)
    routes_keys = jax.random.split(jax.random.fold_in(keys[10], 1), TOTAL_ROWS // ROWS_GRP)
    routes_turns = jax.random.permutation(jax.random.fold_in(keys[10], 3), TOTAL_ROWS // ROWS_GRP)
    routes = jax.vmap(lambda own, number: deal_out(jax.random.fold_in(keys[10], 2), own, number, ROWS_GRP, EXPERTS, TOP, CAP, 2))(routes_keys, routes_turns).reshape((TOTAL_ROWS, TOP))
    w_gate = gaussian(keys[11], (EXPERTS * 2, D, FF // 2), D ** -0.5, 0.09375, ((0, 32),))
    w_up = gaussian(keys[12], (EXPERTS * 2, D, FF // 2), D ** -0.5, 0.09375, ((0, 32),))
    w_down = gaussian(keys[13], (EXPERTS * 2, FF // 2, D), FF ** -0.5, 0.15625, ((0, 32),))
    return dict(query=query, cached_key_block=cached_key_block, cached_value_block=cached_value_block, fresh_token_key=fresh_token_key, fresh_token_value=fresh_token_value, lengths=lengths, residual_in=residual_in, o_weight=o_weight, norm_gain=norm_gain, gate_logits=gate_logits, routes=routes, w_gate=w_gate, w_up=w_up, w_down=w_down)


def reference(query, cached_key_block, cached_value_block, fresh_token_key, fresh_token_value, lengths, residual_in, o_weight, norm_gain, gate_logits, routes, w_gate, w_up, w_down):
    query_group = QUERY_HEADS // KEY_VALUE_HEADS
    softmax_scale = 1.0 / HEAD_SIZE ** 0.5
    highest_score = lax.Precision.HIGHEST
    query_rows = query.astype(jnp.float32).reshape(TOTAL_ROWS, KEY_VALUE_HEADS, query_group, HEAD_SIZE)
    gathered_keys = cached_key_block.astype(jnp.float32).reshape(TOTAL_ROWS, CACHE_LENGTH, KEY_VALUE_HEADS, HEAD_SIZE)
    gathered_values = cached_value_block.astype(jnp.float32).reshape(TOTAL_ROWS, CACHE_LENGTH, KEY_VALUE_HEADS, HEAD_SIZE)
    scores = jnp.einsum('rkgd,rpkd->rkgp', query_rows, gathered_keys, precision=highest_score) * softmax_scale
    self_token_score = jnp.einsum('sznj,szj->szn', query_rows, fresh_token_key.astype(jnp.float32).reshape(TOTAL_ROWS, KEY_VALUE_HEADS, HEAD_SIZE), precision=highest_score) * softmax_scale
    valid = (jnp.arange(CACHE_LENGTH, dtype=jnp.int32)[None, :] < lengths[:, None])[:, None, None, :]
    masked = jnp.where(valid, scores, -1e+30)
    top_score = jnp.maximum(lax.optimization_barrier(jnp.max(masked, axis=-1)), self_token_score)
    weights = jnp.where(valid, jnp.exp(masked - top_score[..., None]), 0.0)
    self_token_weight = jnp.exp(self_token_score - top_score)
    total_all = lax.optimization_barrier(jnp.sum(weights, axis=-1)) + self_token_weight
    summed_output = jnp.einsum('rkgp,rpkd->rkgd', weights, gathered_values, precision=highest_score)
    summed_output = summed_output + self_token_weight[..., None] * fresh_token_value.astype(jnp.float32).reshape(TOTAL_ROWS, KEY_VALUE_HEADS, 1, HEAD_SIZE)
    attended = (summed_output / total_all[..., None]).reshape(TOTAL_ROWS, QUERY_HEADS * HEAD_SIZE).astype(jnp.bfloat16)
    projected = jnp.dot(attended, o_weight, preferred_element_type=jnp.float32)
    stream = residual_in.astype(jnp.float32) + projected
    normed = (stream * lax.rsqrt(lax.optimization_barrier(jnp.mean(stream * stream, axis=-1, keepdims=True)) + 1e-06) * norm_gain).astype(jnp.bfloat16)
    gates = jax.nn.softmax(gate_logits, axis=-1)
    expert_ids = jnp.arange(EXPERTS, dtype=jnp.int32)
    matches = routes[:, :, None] == expert_ids[None, None, :]
    coeffs = lax.optimization_barrier(jnp.sum(jnp.where(matches, gates[:, :, None], 0.0), axis=1))
    hit_rows = jnp.any(matches, axis=1).astype(jnp.int32)
    room = CAP * N_EXPERT
    gate_full = jnp.transpose(w_gate.reshape(EXPERTS, 2, D, FF // 2), (0, 2, 1, 3)).reshape(EXPERTS, D, FF)
    up_full = jnp.transpose(w_up.reshape(EXPERTS, 2, D, FF // 2), (0, 2, 1, 3)).reshape(EXPERTS, D, FF)
    down_full = w_down.reshape(EXPERTS, FF, D)

    def per_expert(carry, inputs):
        hit_col, coeff_col, gate_mat, up_mat, down_mat = inputs
        order = jnp.argsort(1 - hit_col, stable=True)[:room].astype(jnp.int32)
        picked = normed[order]
        gate_act = jnp.dot(picked, gate_mat, preferred_element_type=jnp.float32)
        up_act = jnp.dot(picked, up_mat, preferred_element_type=jnp.float32)
        hidden = (jax.nn.silu(gate_act) * up_act).astype(jnp.bfloat16)
        result = jnp.dot(hidden, down_mat, preferred_element_type=jnp.float32)
        carry = carry.at[order].add(coeff_col[order][:, None] * result)
        return (carry, None)
    start_sum = jnp.zeros((TOTAL_ROWS, D), jnp.float32)
    mixed, _ = lax.scan(per_expert, start_sum, (hit_rows.T, coeffs.T, gate_full, up_full, down_full))
    return (stream + mixed).astype(jnp.bfloat16)
```

```python
import functools
import math

import jax
import jax.numpy as jnp
from jax import lax
from jax.experimental import pallas as pl
from jax.experimental.pallas import tpu as pltpu
from jax.sharding import PartitionSpec as P

KEY_VALUE_HEADS = 4
HEAD_SIZE = 128
MESH = pl.DeviceIdType.MESH
UP_SLOTS = 8
DOWN_SLOTS = 2
BF = jnp.bfloat16
F32 = jnp.float32


def layer_kernel(
    S, E, R, HEADS, D, FH, PIECES, NA, NB,
    len_ref, q_ref, fk_ref, fv_ref, res_ref, gain_ref, logit_ref, route_ref,
    k_hbm, v_hbm, ow_hbm, wg_hbm, wu_hbm, wd_hbm,
    out_ref,
    kbuf, vbuf, owbuf, abuf, bbuf,
    sbuf1, rbuf1, att, sbuf2, rbuf2, strm, xsend, xg, xs, acc, cbuf, rc,
    kv_sem, ow_sem, a_sem, b_sem,
    ss1, rs1, ss2, rs2, ss3, rs3, ss4, rs4,
):
    N = S * E
    T = E * R
    W = D // S
    HD = HEADS // S
    KVH = KEY_VALUE_HEADS
    HS = HEAD_SIZE
    GROUP = HEADS // KVH
    SPAN = kbuf.shape[1]
    HALF = D // 2
    TA = PIECES * 4
    seq = lax.axis_index("seq")
    exp = lax.axis_index("expert")
    me = seq * E + exp

    barrier = pltpu.get_barrier_semaphore()

    def greet(j, _):
        t = lax.rem(me + j, N)
        pl.semaphore_signal(
            barrier, inc=1, device_id={"seq": t // E, "expert": lax.rem(t, E)}, device_id_type=MESH
        )
        return 0

    lax.fori_loop(1, N, greet, 0)

    k_copy = pltpu.make_async_copy(k_hbm, kbuf, kv_sem.at[0])
    v_copy = pltpu.make_async_copy(v_hbm, vbuf, kv_sem.at[1])
    ow_copy = pltpu.make_async_copy(ow_hbm, owbuf, ow_sem.at[0])

    def a_copy(p, i, slot):
        src = wg_hbm if i % 2 == 0 else wu_hbm
        return pltpu.make_async_copy(
            src.at[p, pl.ds((i // 2) * HALF, HALF), :], abuf.at[slot], a_sem.at[slot]
        )

    def b_copy(p, slot):
        return pltpu.make_async_copy(wd_hbm.at[p], bbuf.at[slot], b_sem.at[slot])

    k_copy.start()
    v_copy.start()
    ow_copy.start()
    for p in range(PIECES):
        for i in range(4):
            if p * 4 + i < NA:
                a_copy(p, i, p * 4 + i).start()
        if p < NB:
            b_copy(p, p).start()

    scale = 1.0 / math.sqrt(HS)
    head_row = lax.broadcasted_iota(jnp.int32, (HEADS, KVH * HS), 0) // GROUP
    head_col = lax.broadcasted_iota(jnp.int32, (HEADS, KVH * HS), 1) // HS
    diag = head_row == head_col
    position = seq * SPAN + lax.broadcasted_iota(jnp.int32, (HEADS, SPAN), 1)
    lane = lax.broadcasted_iota(jnp.int32, (HEADS, HS), 1)
    has_own = seq == 0

    def spread(row):
        return jnp.concatenate(
            [jnp.broadcast_to(row[:, k * HS : (k + 1) * HS], (GROUP, HS)) for k in range(KVH)], axis=0
        )

    k_copy.wait()
    scores = []
    for r in range(R):
        q = q_ref[r]
        wide = jnp.where(diag, jnp.concatenate([q] * KVH, axis=1), jnp.zeros((), BF))
        scores.append(
            lax.dot_general(wide, kbuf[r], (((1,), (1,)), ((), ())), preferred_element_type=F32) * scale
        )
    v_copy.wait()
    fk = fk_ref[...].astype(F32)
    fv = fv_ref[...].astype(F32)
    packed = jnp.zeros((HEADS, HS), F32)
    for r in range(R):
        valid = position < len_ref[r]
        masked = jnp.where(valid, scores[r], -1e30)
        own = jnp.sum(q_ref[r].astype(F32) * spread(fk[r : r + 1]), axis=1, keepdims=True) * scale
        own = jnp.where(has_own, own, -1e30)
        peak = jnp.maximum(jnp.max(masked, axis=1, keepdims=True), own)
        weight = jnp.where(valid, jnp.exp(masked - peak), 0.0)
        own_weight = jnp.where(has_own, jnp.exp(own - peak), 0.0)
        total = jnp.sum(weight, axis=1, keepdims=True) + own_weight
        high = weight.astype(BF)
        low = (weight - high.astype(F32)).astype(BF)
        both = jnp.dot(jnp.concatenate([high, low], axis=0), vbuf[r], preferred_element_type=F32)
        both = both[:HEADS] + both[HEADS:]
        summed = jnp.concatenate(
            [both[k * GROUP : (k + 1) * GROUP, k * HS : (k + 1) * HS] for k in range(KVH)], axis=0
        )
        summed = summed + own_weight * spread(fv[r : r + 1])
        packed = jnp.where(lane == r, peak, jnp.where(lane == R + r, total, packed))
        for s in range(S):
            sbuf1[s, r] = summed[s * HD : (s + 1) * HD]
    for s in range(S):
        sbuf1[s, R] = packed[s * HD : (s + 1) * HD]

    pl.semaphore_wait(barrier, N - 1)

    def copy1(j):
        peer = lax.rem(seq + j, S)
        return pltpu.make_async_remote_copy(
            src_ref=sbuf1.at[peer], dst_ref=rbuf1.at[j], send_sem=ss1.at[j], recv_sem=rs1.at[j],
            device_id={"seq": peer, "expert": exp}, device_id_type=MESH,
        )

    def start1(j, _):
        copy1(j).start()
        return 0

    def wait1(j, _):
        copy1(j).wait_recv()
        return 0

    lax.fori_loop(1, S, start1, 0)
    rbuf1[0] = sbuf1[seq]
    lax.fori_loop(1, S, wait1, 0)

    stats = rbuf1[:, R]
    for r in range(R):
        peak = stats[:, :, r : r + 1]
        total = stats[:, :, R + r : R + r + 1]
        factor = jnp.exp(peak - jnp.max(peak, axis=0, keepdims=True))
        att[r] = jnp.sum(factor * rbuf1[:, r], axis=0) / jnp.sum(factor * total, axis=0)
    attended = jnp.concatenate([att[:, h, :] for h in range(HD)], axis=1).astype(BF)

    ow_copy.wait()

    def copy2(j):
        peer = lax.rem(seq + j, S)
        return pltpu.make_async_remote_copy(
            src_ref=sbuf2.at[j], dst_ref=rbuf2.at[j], send_sem=ss2.at[j], recv_sem=rs2.at[j],
            device_id={"seq": peer, "expert": exp}, device_id_type=MESH,
        )

    def project(j):
        cols = pl.ds(pl.multiple_of(lax.rem(seq + j, S) * W, W), W)
        return jnp.dot(attended, owbuf[:, cols], preferred_element_type=F32)

    def start2(j, _):
        sbuf2[j] = project(j)
        copy2(j).start()
        return 0

    def wait2(j, _):
        copy2(j).wait_recv()
        return 0

    lax.fori_loop(1, S, start2, 0)
    rbuf2[0] = project(0)
    lax.fori_loop(1, S, wait2, 0)

    own_cols = pl.ds(pl.multiple_of(seq * W, W), W)
    stream = res_ref[:, own_cols].astype(F32) + jnp.sum(rbuf2[...], axis=0)
    strm[...] = stream
    squares = jnp.sum(stream * stream, axis=1, keepdims=True)
    part0 = squares.astype(BF).astype(F32)
    part1 = (squares - part0).astype(BF).astype(F32)
    part2 = squares - part0 - part1
    lane_r = lax.broadcasted_iota(jnp.int32, (R, 128), 1)
    tail = jnp.where(
        lane_r == 0, part0, jnp.where(lane_r == 1, part1, jnp.where(lane_r == 2, part2, 0.0))
    )
    xsend[...] = jnp.concatenate([stream * gain_ref[:, own_cols], tail], axis=1).astype(BF)

    def target(j):
        t = lax.rem(me + j, N)
        return t // E, lax.rem(t, E)

    def copy3(j, dst):
        ts, te = target(j)
        return pltpu.make_async_remote_copy(
            src_ref=xsend, dst_ref=dst, send_sem=ss3.at[j], recv_sem=rs3.at[j],
            device_id={"seq": ts, "expert": te}, device_id_type=MESH,
        )

    def start3(j, _):
        copy3(j, xg.at[seq, exp]).start()
        return 0

    def wait3(j, _):
        ts, te = target(N - j)
        copy3(j, xg.at[ts, te]).wait_recv()
        return 0

    lax.fori_loop(1, N, start3, 0)
    xg[seq, exp] = xsend[...]

    logits = logit_ref[...]
    odds = jnp.exp(logits - jnp.max(logits, axis=1, keepdims=True))
    gates = odds / jnp.sum(odds, axis=1, keepdims=True)

    lax.fori_loop(1, N, wait3, 0)
    squares = jnp.zeros((T, 1), F32)
    for s in range(S):
        block = xg[s].astype(F32).reshape(T, W + 128)
        xs[(s * W) // HALF, :, (s * W) % HALF : (s * W) % HALF + W] = block[:, :W].astype(BF)
        squares = squares + jnp.sum(block[:, W:], axis=1, keepdims=True)
    inverse = lax.rsqrt(squares * (1.0 / D) + 1e-6)

    def copy4(c, e):
        return pltpu.make_async_remote_copy(
            src_ref=cbuf.at[c, e], dst_ref=rc.at[me], send_sem=ss4.at[c * E + e], recv_sem=rs4.at[me],
            device_id={"seq": c, "expert": e}, device_id_type=MESH,
        )

    def piece(p, _):
        acts = []
        for half in range(2):
            for m in range(2):
                i = half * 2 + m
                unit = p * 4 + i
                slot = lax.rem(unit, NA)
                a_copy(p, i, slot).wait()
                part = jnp.dot(xs[half], abuf[slot], preferred_element_type=F32)
                if half == 0:
                    acts.append(part)
                else:
                    acts[m] = acts[m] + part
                if TA > NA:

                    @pl.when(unit + NA < TA)
                    def _():
                        a_copy(p + NA // 4, i, slot).start()

        gate_act = acts[0] * inverse
        up_act = acts[1] * inverse
        hidden = (gate_act / (1.0 + jnp.exp(-gate_act)) * up_act).astype(BF)
        expert_id = (me * PIECES + p) // 2
        coeff = jnp.sum(jnp.where(route_ref[...] == expert_id, gates, 0.0), axis=1, keepdims=True)
        slot = lax.rem(p, NB)
        b_copy(p, slot).wait()

        def columns(j, _):
            c = lax.rem(seq + j, S)
            cols = pl.ds(pl.multiple_of(c * W, W), W)
            result = coeff * jnp.dot(hidden, bbuf[slot, :, cols], preferred_element_type=F32)

            @pl.when(p == 0)
            def _():
                acc[c] = result

            @pl.when(p > 0)
            def _():
                acc[c] = acc[c] + result

            @pl.when(p == PIECES - 1)
            def _():
                value = acc[c]
                for e in range(E):
                    cbuf[c, e] = value[e * R : (e + 1) * R].astype(BF)

                    @pl.when(c * E + e != me)
                    def _():
                        copy4(c, e).start()

            return 0

        lax.fori_loop(1, S + 1, columns, 0)
        if PIECES > NB:

            @pl.when(p + NB < PIECES)
            def _():
                b_copy(p + NB, slot).start()

        return 0

    lax.fori_loop(0, PIECES, piece, 0)
    rc[me] = cbuf[seq, exp]

    def wait4(j, _):
        ts, te = target(j)
        src = ts * E + te
        pltpu.make_async_remote_copy(
            src_ref=cbuf.at[ts, te], dst_ref=rc.at[src], send_sem=ss4.at[src], recv_sem=rs4.at[src],
            device_id={"seq": ts, "expert": te}, device_id_type=MESH,
        ).wait_recv()
        return 0

    lax.fori_loop(1, N, wait4, 0)
    out_ref[...] = (strm[...] + jnp.sum(rc[...].astype(F32), axis=0)).astype(BF)

    def sent12(j, _):
        copy1(j).wait_send()
        copy2(j).wait_send()
        return 0

    def sent34(j, _):
        copy3(j, xg.at[seq, exp]).wait_send()
        ts, te = target(j)
        copy4(ts, te).wait_send()
        return 0

    lax.fori_loop(1, S, sent12, 0)
    lax.fori_loop(1, N, sent34, 0)


def on_device(
    query, cached_key_block, cached_value_block, fresh_token_key, fresh_token_value, lengths,
    residual_in, o_weight, norm_gain, gate_logits, routes, w_gate, w_up, w_down,
):
    S, E = lax.axis_size("seq"), lax.axis_size("expert")
    R, D = residual_in.shape
    HEADS = query.shape[1] // HEAD_SIZE
    SPAN = cached_key_block.shape[1]
    KV = cached_key_block.shape[2]
    PIECES, _, FH = w_gate.shape
    N, T, W, HD = S * E, E * R, D // S, HEADS // S
    NA, NB = min(UP_SLOTS, PIECES * 4), min(DOWN_SLOTS, PIECES)
    vmem = pl.BlockSpec(memory_space=pltpu.VMEM)
    hbm = pl.BlockSpec(memory_space=pl.ANY)
    dma = pltpu.SemaphoreType.DMA
    read = 2 * (w_gate.size + w_up.size + w_down.size + o_weight.size + 2 * cached_key_block.size)
    return pl.pallas_call(
        functools.partial(layer_kernel, S, E, R, HEADS, D, FH, PIECES, NA, NB),
        out_shape=jax.ShapeDtypeStruct((R, W), BF),
        in_specs=[pl.BlockSpec(memory_space=pltpu.SMEM)] + [vmem] * 7 + [hbm] * 6,
        out_specs=vmem,
        scratch_shapes=[
            pltpu.VMEM((R, SPAN, KV), BF),
            pltpu.VMEM((R, SPAN, KV), BF),
            pltpu.VMEM(o_weight.shape, BF),
            pltpu.VMEM((NA, D // 2, FH), BF),
            pltpu.VMEM((NB, FH, D), BF),
            pltpu.VMEM((S, R + 1, HD, HEAD_SIZE), F32),
            pltpu.VMEM((S, R + 1, HD, HEAD_SIZE), F32),
            pltpu.VMEM((R, HD, HEAD_SIZE), F32),
            pltpu.VMEM((S, R, W), F32),
            pltpu.VMEM((S, R, W), F32),
            pltpu.VMEM((R, W), F32),
            pltpu.VMEM((R, W + 128), BF),
            pltpu.VMEM((S, E, R, W + 128), BF),
            pltpu.VMEM((2, T, D // 2), BF),
            pltpu.VMEM((S, T, W), F32),
            pltpu.VMEM((S, E, R, W), BF),
            pltpu.VMEM((N, R, W), BF),
            dma((2,)), dma((1,)), dma((NA,)), dma((NB,)),
            dma((S,)), dma((S,)), dma((S,)), dma((S,)),
            dma((N,)), dma((N,)), dma((N,)), dma((N,)),
        ],
        compiler_params=pltpu.CompilerParams(
            collective_id=0, has_side_effects=True, vmem_limit_bytes=60 * 1024 * 1024
        ),
        cost_estimate=pl.CostEstimate(flops=T * read, bytes_accessed=read, transcendentals=0),
    )(
        lengths, query.reshape(R, HEADS, HEAD_SIZE), fresh_token_key, fresh_token_value, residual_in,
        norm_gain.reshape(1, D), gate_logits, routes,
        cached_key_block, cached_value_block, o_weight, w_gate, w_up, w_down,
    )


def solution(mesh):
    placed = (
        P("expert", None),
        P("expert", "seq", None),
        P("expert", "seq", None),
        P("expert", None),
        P("expert", None),
        P("expert"),
        P("expert", None),
        P("seq", None),
        P(),
        P(),
        P(),
        P(("seq", "expert"), None, None),
        P(("seq", "expert"), None, None),
        P(("seq", "expert"), None, None),
    )
    return jax.shard_map(
        on_device, mesh=mesh, in_specs=placed, out_specs=P("expert", "seq"), check_vma=False
    )
```

```python
import functools
import math

import jax
import jax.numpy as jnp
from jax import lax
from jax.experimental import pallas as pl
from jax.experimental.pallas import tpu as pltpu
from jax.sharding import PartitionSpec as P

KEY_VALUE_HEADS = 4
HEAD_SIZE = 128
MESH = pl.DeviceIdType.MESH
CAP = 2
UP_SLOTS = 12
DOWN_SLOTS = 2
BF = jnp.bfloat16
F32 = jnp.float32


def split3(value):
    first = value.astype(BF).astype(F32)
    second = (value - first).astype(BF).astype(F32)
    return [first, second, (value - first - second).astype(BF).astype(F32)]


def layer_kernel(
    S, E, R, HEADS, D, FH, PIECES, NA, NB,
    len_ref, q_ref, fk_ref, fv_ref, res_ref, gain_ref, logit_ref, route_ref,
    k_hbm, v_hbm, ow_hbm, wg_hbm, wu_hbm, wd_hbm,
    out_ref,
    kbuf, vbuf, owbuf, abuf, bbuf,
    qbuf, sbuf1, rbuf1, att, sbuf2, rbuf2, strm, xsend, xg, xs, acc, cbuf, rc,
    kv_sem, ow_sem, a_sem, b_sem,
    ss1, rs1, ss2, rs2, ss3, rs3, ss4, rs4,
):
    N = S * E
    T = E * R
    LOCAL = max(1, PIECES // 2)
    L = LOCAL * CAP
    M = E * L
    NL = N * L
    W = D // S
    HD = HEADS // S
    KVH = KEY_VALUE_HEADS
    HS = HEAD_SIZE
    GROUP = HEADS // KVH
    SPAN = kbuf.shape[1]
    HALF = D // 2
    TA = PIECES * 4
    REUSE = PIECES > NB and owbuf.shape[0] >= FH
    seq = lax.axis_index("seq")
    exp = lax.axis_index("expert")
    me = seq * E + exp

    barrier = pltpu.get_barrier_semaphore()

    def greet(j, _):
        t = lax.rem(me + j, N)
        pl.semaphore_signal(
            barrier, inc=1, device_id={"seq": t // E, "expert": lax.rem(t, E)}, device_id_type=MESH
        )
        return 0

    lax.fori_loop(1, N, greet, 0)

    k_copy = pltpu.make_async_copy(k_hbm, kbuf, kv_sem.at[0])
    v_copy = pltpu.make_async_copy(v_hbm, vbuf, kv_sem.at[1])
    ow_copy = pltpu.make_async_copy(ow_hbm, owbuf, ow_sem.at[0])

    def a_copy(p, i, slot):
        src = wg_hbm if i % 2 == 0 else wu_hbm
        return pltpu.make_async_copy(
            src.at[p, pl.ds((i // 2) * HALF, HALF), :], abuf.at[slot], a_sem.at[slot]
        )

    def b_copy(p, slot):
        return pltpu.make_async_copy(wd_hbm.at[p], bbuf.at[slot], b_sem.at[slot])

    k_copy.start()
    v_copy.start()
    ow_copy.start()
    for p in range(PIECES):
        for i in range(4):
            if p * 4 + i < NA:
                a_copy(p, i, p * 4 + i).start()
        if p < NB:
            b_copy(p, p).start()

    scale = 1.0 / math.sqrt(HS)
    head_row = lax.broadcasted_iota(jnp.int32, (HEADS, KVH * HS), 0) // GROUP
    head_col = lax.broadcasted_iota(jnp.int32, (HEADS, KVH * HS), 1) // HS
    diag = head_row == head_col
    position = seq * SPAN + lax.broadcasted_iota(jnp.int32, (HEADS, SPAN), 1)
    lane = lax.broadcasted_iota(jnp.int32, (HEADS, HS), 1)
    has_own = seq == 0

    def joined(parts, i, r):
        cut = [parts[:, :, (i + k) * R + r : (i + k) * R + r + 1] for k in range(3)]
        return cut[0] + cut[1] + cut[2]

    def spread(row):
        return jnp.concatenate(
            [jnp.broadcast_to(row[:, k * HS : (k + 1) * HS], (GROUP, HS)) for k in range(KVH)], axis=0
        )

    for h in range(HEADS):
        qbuf[h] = q_ref[:, h * HS : (h + 1) * HS].astype(F32)
    queries = [qbuf[:, r, :] for r in range(R)]
    k_copy.wait()
    scores = []
    for r in range(R):
        q = queries[r].astype(BF)
        wide = jnp.where(diag, jnp.concatenate([q] * KVH, axis=1), jnp.zeros((), BF))
        scores.append(
            lax.dot_general(wide, kbuf[r], (((1,), (1,)), ((), ())), preferred_element_type=F32) * scale
        )
    v_copy.wait()
    fk = fk_ref[...].astype(F32)
    fv = fv_ref[...].astype(F32)
    packed = jnp.zeros((HEADS, HS), F32)
    for r in range(R):
        valid = position < len_ref[r]
        masked = jnp.where(valid, scores[r], -1e30)
        own = jnp.sum(queries[r] * spread(fk[r : r + 1]), axis=1, keepdims=True) * scale
        own = jnp.where(has_own, own, -1e30)
        peak = jnp.maximum(jnp.max(masked, axis=1, keepdims=True), own)
        weight = jnp.where(valid, jnp.exp(masked - peak), 0.0)
        own_weight = jnp.where(has_own, jnp.exp(own - peak), 0.0)
        total = jnp.sum(weight, axis=1, keepdims=True) + own_weight
        high = weight.astype(BF)
        low = (weight - high.astype(F32)).astype(BF)
        both = jnp.dot(jnp.concatenate([high, low], axis=0), vbuf[r], preferred_element_type=F32)
        both = both[:HEADS] + both[HEADS:]
        summed = jnp.concatenate(
            [both[k * GROUP : (k + 1) * GROUP, k * HS : (k + 1) * HS] for k in range(KVH)], axis=0
        )
        summed = summed + own_weight * spread(fv[r : r + 1])
        for i, part in enumerate(split3(peak) + split3(total)):
            packed = jnp.where(lane == i * R + r, part, packed)
        for s in range(S):
            sbuf1[s, r] = summed[s * HD : (s + 1) * HD].astype(BF)
    for s in range(S):
        sbuf1[s, R] = packed[s * HD : (s + 1) * HD].astype(BF)

    logits = logit_ref[...]
    odds = jnp.exp(logits - jnp.max(logits, axis=0, keepdims=True))
    gates = odds / jnp.sum(odds, axis=0, keepdims=True)
    routes = route_ref[...]
    slot_id = lax.broadcasted_iota(jnp.int32, (NL, T), 0)
    place = slot_id % L
    slot_expert = ((slot_id // L) * PIECES) // 2 + place // CAP
    row_id = lax.broadcasted_iota(jnp.int32, (NL, T), 1)
    hits = jnp.zeros((NL, T), F32)
    share = jnp.zeros((NL, T), F32)
    for k in range(routes.shape[0]):
        match = (routes[k : k + 1] == slot_expert) & (row_id // R == exp)
        hits = jnp.where(match, 1.0, hits)
        share = share + jnp.where(match, gates[k : k + 1], 0.0)
    earlier = lax.broadcasted_iota(jnp.int32, (T, T), 0) < lax.broadcasted_iota(jnp.int32, (T, T), 1)
    before = jnp.dot(
        hits.astype(BF), jnp.where(earlier, 1.0, 0.0).astype(BF), preferred_element_type=F32
    )
    taken = (hits > 0.5) & (before == (place % CAP).astype(F32))
    chosen = jnp.where(taken, 1.0, 0.0)
    share = jnp.where(taken, share, 0.0)

    pl.semaphore_wait(barrier, N - 1)

    def copy1(j):
        peer = lax.rem(seq + j, S)
        return pltpu.make_async_remote_copy(
            src_ref=sbuf1.at[peer], dst_ref=rbuf1.at[j], send_sem=ss1.at[j], recv_sem=rs1.at[j],
            device_id={"seq": peer, "expert": exp}, device_id_type=MESH,
        )

    def start1(j, _):
        copy1(j).start()
        return 0

    def wait1(j, _):
        copy1(j).wait_recv()
        return 0

    lax.fori_loop(1, S, start1, 0)
    rbuf1[0] = sbuf1[seq]
    lax.fori_loop(1, S, wait1, 0)

    stats = rbuf1[:, R].astype(F32)
    for r in range(R):
        peak = joined(stats, 0, r)
        total = joined(stats, 3, r)
        factor = jnp.exp(peak - jnp.max(peak, axis=0, keepdims=True))
        att[r] = jnp.sum(factor * rbuf1[:, r].astype(F32), axis=0) / jnp.sum(factor * total, axis=0)
    attended = jnp.concatenate([att[:, h, :] for h in range(HD)], axis=1).astype(BF)

    ow_copy.wait()

    def copy2(j):
        peer = lax.rem(seq + j, S)
        return pltpu.make_async_remote_copy(
            src_ref=sbuf2.at[j], dst_ref=rbuf2.at[j], send_sem=ss2.at[j], recv_sem=rs2.at[j],
            device_id={"seq": peer, "expert": exp}, device_id_type=MESH,
        )

    def project(j):
        cols = pl.ds(pl.multiple_of(lax.rem(seq + j, S) * W, W), W)
        return jnp.dot(attended, owbuf[:, cols], preferred_element_type=F32)

    def start2(j, _):
        sbuf2[j] = project(j).astype(BF)
        copy2(j).start()
        return 0

    def wait2(j, _):
        copy2(j).wait_recv()
        return 0

    lax.fori_loop(1, S, start2, 0)
    own_projected = project(0)
    rbuf2[0] = jnp.zeros((R, W), BF)
    if REUSE:
        pltpu.make_async_copy(wd_hbm.at[NB], owbuf.at[pl.ds(0, FH), :], b_sem.at[NB]).start()
    lax.fori_loop(1, S, wait2, 0)

    own_cols = pl.ds(pl.multiple_of(seq * W, W), W)
    stream = res_ref[:, own_cols].astype(F32) + own_projected + jnp.sum(rbuf2[...].astype(F32), axis=0)
    strm[...] = stream
    squares = jnp.sum(stream * stream, axis=1, keepdims=True)
    parts = split3(squares)
    lane_r = lax.broadcasted_iota(jnp.int32, (R, 128), 1)
    tail = jnp.zeros((R, 128), F32)
    for i in range(3):
        tail = jnp.where(lane_r == i, parts[i], tail)
    sent = jnp.concatenate([stream * gain_ref[:, own_cols], tail], axis=1)
    slots = jnp.dot(
        chosen.astype(BF), jnp.concatenate([sent] * E, axis=0).astype(BF), preferred_element_type=F32
    )
    for t in range(N):
        xsend[t] = slots[t * L : (t + 1) * L].astype(BF)

    def target(j):
        t = lax.rem(me + j, N)
        return t // E, lax.rem(t, E)

    def copy3(j, dst):
        ts, te = target(j)
        return pltpu.make_async_remote_copy(
            src_ref=xsend.at[ts * E + te], dst_ref=dst, send_sem=ss3.at[j], recv_sem=rs3.at[j],
            device_id={"seq": ts, "expert": te}, device_id_type=MESH,
        )

    def start3(j, _):
        copy3(j, xg.at[seq, exp]).start()
        return 0

    def wait3(j, _):
        ts, te = target(N - j)
        copy3(j, xg.at[ts, te]).wait_recv()
        return 0

    lax.fori_loop(1, N, start3, 0)
    xg[seq, exp] = xsend[me]

    lax.fori_loop(1, N, wait3, 0)
    squares = jnp.zeros((M, 1), F32)
    for s in range(S):
        block = jnp.concatenate([xg[s, e].astype(F32) for e in range(E)], axis=0)
        xs[(s * W) // HALF, :, (s * W) % HALF : (s * W) % HALF + W] = block[:, :W].astype(BF)
        squares = squares + jnp.sum(block[:, W:], axis=1, keepdims=True)
    inverse = lax.rsqrt(squares * (1.0 / D) + 1e-6)

    def copy4(c, e):
        return pltpu.make_async_remote_copy(
            src_ref=cbuf.at[c, e], dst_ref=rc.at[me], send_sem=ss4.at[c * E + e], recv_sem=rs4.at[me],
            device_id={"seq": c, "expert": e}, device_id_type=MESH,
        )

    def piece(p, _):
        acts = []
        for half in range(2):
            for m in range(2):
                i = half * 2 + m
                unit = p * 4 + i
                slot = lax.rem(unit, NA)
                a_copy(p, i, slot).wait()
                part = jnp.zeros((M, FH), F32)
                for k in range(0, HALF, 512):
                    part = part + jnp.dot(
                        xs[half, :, k : k + 512], abuf[slot, k : k + 512, :], preferred_element_type=F32
                    )
                if half == 0:
                    acts.append(part)
                else:
                    acts[m] = acts[m] + part
                if TA > NA:

                    @pl.when(unit + NA < TA)
                    def _():
                        a_copy(p + NA // 4, i, slot).start()

        gate_act = acts[0] * inverse
        up_act = acts[1] * inverse
        hidden = (gate_act / (1.0 + jnp.exp(-gate_act)) * up_act).astype(BF)
        local = (lax.broadcasted_iota(jnp.int32, (M, W), 0) % L) // CAP == p // 2
        def combine(view):
            def columns(j, _):
                c = lax.rem(seq + j, S)
                cols = pl.ds(pl.multiple_of(c * W, W), W)
                result = jnp.dot(hidden, view[pl.ds(0, FH), cols], preferred_element_type=F32)
                result = jnp.where(local, result, 0.0)

                @pl.when(p == 0)
                def _():
                    acc[c] = result

                @pl.when(p > 0)
                def _():
                    acc[c] = acc[c] + result

                @pl.when(p == PIECES - 1)
                def _():
                    value = acc[c]
                    for e in range(E):
                        cbuf[c, e] = value[e * L : (e + 1) * L].astype(BF)

                        @pl.when(c * E + e != me)
                        def _():
                            copy4(c, e).start()

                return 0

            lax.fori_loop(1, S + 1, columns, 0)

        slot = lax.rem(p - p // (NB + 1), NB)
        if REUSE:

            @pl.when(p == NB)
            def _():
                pltpu.make_async_copy(wd_hbm.at[p], owbuf.at[pl.ds(0, FH), :], b_sem.at[NB]).wait()
                combine(owbuf)

            @pl.when(p != NB)
            def _():
                b_copy(p, slot).wait()
                combine(bbuf.at[slot])

            @pl.when((p < NB) & (p + NB + 1 < PIECES))
            def _():
                b_copy(p + NB + 1, slot).start()

        else:
            b_copy(p, slot).wait()
            combine(bbuf.at[slot])
        return 0

    lax.fori_loop(0, PIECES, piece, 0)
    rc[me] = cbuf[seq, exp]

    def wait4(j, _):
        ts, te = target(j)
        src = ts * E + te
        pltpu.make_async_remote_copy(
            src_ref=cbuf.at[ts, te], dst_ref=rc.at[src], send_sem=ss4.at[src], recv_sem=rs4.at[src],
            device_id={"seq": ts, "expert": te}, device_id_type=MESH,
        ).wait_recv()
        return 0

    lax.fori_loop(1, N, wait4, 0)
    back = jnp.concatenate([rc[t].astype(F32) for t in range(N)], axis=0).astype(BF)
    share_high = share.astype(BF)
    share_low = (share - share_high.astype(F32)).astype(BF)
    turned = (((0,), (0,)), ((), ()))
    added = lax.dot_general(share_high, back, turned, preferred_element_type=F32)
    added = added + lax.dot_general(share_low, back, turned, preferred_element_type=F32)
    total = strm[...]
    for e in range(E):
        total = total + added[e * R : (e + 1) * R]
    out_ref[...] = total.astype(BF)

    def sent12(j, _):
        copy1(j).wait_send()
        copy2(j).wait_send()
        return 0

    def sent34(j, _):
        copy3(j, xg.at[seq, exp]).wait_send()
        ts, te = target(j)
        copy4(ts, te).wait_send()
        return 0

    lax.fori_loop(1, S, sent12, 0)
    lax.fori_loop(1, N, sent34, 0)


def on_device(
    query, cached_key_block, cached_value_block, fresh_token_key, fresh_token_value, lengths,
    residual_in, o_weight, norm_gain, gate_logits, routes, w_gate, w_up, w_down,
):
    S, E = lax.axis_size("seq"), lax.axis_size("expert")
    R, D = residual_in.shape
    HEADS = query.shape[1] // HEAD_SIZE
    SPAN = cached_key_block.shape[1]
    KV = cached_key_block.shape[2]
    PIECES, _, FH = w_gate.shape
    N, T, W, HD = S * E, E * R, D // S, HEADS // S
    L = max(1, PIECES // 2) * CAP
    M = E * L
    NA, NB = min(UP_SLOTS, PIECES * 4), min(DOWN_SLOTS, PIECES)
    assert PIECES <= 4 and (PIECES <= NB or o_weight.shape[0] >= FH)
    vmem = pl.BlockSpec(memory_space=pltpu.VMEM)
    hbm = pl.BlockSpec(memory_space=pl.ANY)
    dma = pltpu.SemaphoreType.DMA
    read = 2 * (w_gate.size + w_up.size + w_down.size + o_weight.size + 2 * cached_key_block.size)
    return pl.pallas_call(
        functools.partial(layer_kernel, S, E, R, HEADS, D, FH, PIECES, NA, NB),
        out_shape=jax.ShapeDtypeStruct((R, W), BF),
        in_specs=[pl.BlockSpec(memory_space=pltpu.SMEM)] + [vmem] * 7 + [hbm] * 6,
        out_specs=vmem,
        scratch_shapes=[
            pltpu.VMEM((R, SPAN, KV), BF),
            pltpu.VMEM((R, SPAN, KV), BF),
            pltpu.VMEM(o_weight.shape, BF),
            pltpu.VMEM((NA, D // 2, FH), BF),
            pltpu.VMEM((NB, FH, D), BF),
            pltpu.VMEM((HEADS, R, HEAD_SIZE), F32),
            pltpu.VMEM((S, R + 1, HD, HEAD_SIZE), BF),
            pltpu.VMEM((S, R + 1, HD, HEAD_SIZE), BF),
            pltpu.VMEM((R, HD, HEAD_SIZE), F32),
            pltpu.VMEM((S, R, W), BF),
            pltpu.VMEM((S, R, W), BF),
            pltpu.VMEM((R, W), F32),
            pltpu.VMEM((N, L, W + 128), BF),
            pltpu.VMEM((S, E, L, W + 128), BF),
            pltpu.VMEM((2, M, D // 2), BF),
            pltpu.VMEM((S, M, W), F32),
            pltpu.VMEM((S, E, L, W), BF),
            pltpu.VMEM((N, L, W), BF),
            dma((2,)), dma((1,)), dma((NA,)), dma((NB + 1,)),
            dma((S,)), dma((S,)), dma((S,)), dma((S,)),
            dma((N,)), dma((N,)), dma((N,)), dma((N,)),
        ],
        compiler_params=pltpu.CompilerParams(
            collective_id=0, has_side_effects=True, vmem_limit_bytes=63 * 1024 * 1024
        ),
        cost_estimate=pl.CostEstimate(flops=T * read, bytes_accessed=read, transcendentals=0),
    )(
        lengths, query, fresh_token_key, fresh_token_value, residual_in,
        norm_gain.reshape(1, D), gate_logits.T, routes.T,
        cached_key_block, cached_value_block, o_weight, w_gate, w_up, w_down,
    )


def solution(mesh):
    placed = (
        P("expert", None),
        P("expert", "seq", None),
        P("expert", "seq", None),
        P("expert", None),
        P("expert", None),
        P("expert"),
        P("expert", None),
        P("seq", None),
        P(),
        P(),
        P(),
        P(("seq", "expert"), None, None),
        P(("seq", "expert"), None, None),
        P(("seq", "expert"), None, None),
    )
    return jax.shard_map(
        on_device, mesh=mesh, in_specs=placed, out_specs=P("expert", "seq"), check_vma=False
    )
```

```python
import functools
import math

import jax
import jax.numpy as jnp
from jax import lax
from jax.experimental import pallas as pl
from jax.experimental.pallas import tpu as pltpu
from jax.sharding import PartitionSpec as P

KEY_VALUE_HEADS = 4
HEAD_SIZE = 128
MESH = pl.DeviceIdType.MESH
CAP = 2
UP_SLOTS = 8
DOWN_SLOTS = 2
BF = jnp.bfloat16
F32 = jnp.float32


def split3(value):
    first = value.astype(BF).astype(F32)
    second = (value - first).astype(BF).astype(F32)
    return [first, second, (value - first - second).astype(BF).astype(F32)]


def layer_kernel(
    S, E, R, HEADS, D, FH, PIECES, NA, NB,
    len_ref, q_ref, fk_ref, fv_ref, res_ref, gain_ref, logit_ref, route_ref,
    k_hbm, v_hbm, ow_hbm, wg_hbm, wu_hbm, wd_hbm,
    out_ref,
    kbuf, vbuf, owbuf, abuf, bbuf,
    qbuf, sbuf1, rbuf1, att, sbuf2, rbuf2, strm, xsend, xg, xs, acc, cbuf, rc,
    kv_sem, ow_sem, a_sem, b_sem,
    ss1, rs1, ss2, rs2, ss3, rs3, ss4, rs4,
):
    N = S * E
    T = E * R
    LOCAL = max(1, PIECES // 2)
    L = LOCAL * CAP
    M = E * L
    NL = N * L
    W = D // S
    HD = HEADS // S
    KVH = KEY_VALUE_HEADS
    HS = HEAD_SIZE
    GROUP = HEADS // KVH
    SPAN = kbuf.shape[1]
    HALF = D // 2
    TA = PIECES * 4
    REUSE = PIECES > NB and owbuf.shape[0] >= FH
    seq = lax.axis_index("seq")
    exp = lax.axis_index("expert")
    me = seq * E + exp

    barrier = pltpu.get_barrier_semaphore()

    def greet(j, _):
        t = lax.rem(me + j, N)
        pl.semaphore_signal(
            barrier, inc=1, device_id={"seq": t // E, "expert": lax.rem(t, E)}, device_id_type=MESH
        )
        return 0


    k_copy = pltpu.make_async_copy(k_hbm, kbuf, kv_sem.at[0])
    v_copy = pltpu.make_async_copy(v_hbm, vbuf, kv_sem.at[1])
    ow_copy = pltpu.make_async_copy(ow_hbm, owbuf, ow_sem.at[0])

    def a_copy(p, i, slot):
        src = wg_hbm if i % 2 == 0 else wu_hbm
        return pltpu.make_async_copy(
            src.at[p, pl.ds((i // 2) * HALF, HALF), :], abuf.at[slot], a_sem.at[slot]
        )

    def b_copy(p, slot):
        return pltpu.make_async_copy(wd_hbm.at[p], bbuf.at[slot], b_sem.at[slot])

    k_copy.start()
    v_copy.start()
    ow_copy.start()
    for p in range(PIECES):
        for i in range(4):
            if p * 4 + i < NA:
                a_copy(p, i, p * 4 + i).start()
        if p < NB:
            b_copy(p, p).start()

    lax.fori_loop(1, N, greet, 0)

    scale = 1.0 / math.sqrt(HS)
    head_row = lax.broadcasted_iota(jnp.int32, (HEADS, KVH * HS), 0) // GROUP
    head_col = lax.broadcasted_iota(jnp.int32, (HEADS, KVH * HS), 1) // HS
    diag = head_row == head_col
    position = seq * SPAN + lax.broadcasted_iota(jnp.int32, (HEADS, SPAN), 1)
    lane = lax.broadcasted_iota(jnp.int32, (HEADS, HS), 1)
    has_own = seq == 0

    def joined(parts, i, r):
        cut = [parts[:, :, (i + k) * R + r : (i + k) * R + r + 1] for k in range(3)]
        return cut[0] + cut[1] + cut[2]

    def spread(row):
        return jnp.concatenate(
            [jnp.broadcast_to(row[:, k * HS : (k + 1) * HS], (GROUP, HS)) for k in range(KVH)], axis=0
        )

    for h in range(HEADS):
        qbuf[h] = q_ref[:, h * HS : (h + 1) * HS].astype(F32)
    queries = [qbuf[:, r, :] for r in range(R)]
    k_copy.wait()
    scores = []
    for r in range(R):
        q = queries[r].astype(BF)
        wide = jnp.where(diag, jnp.concatenate([q] * KVH, axis=1), jnp.zeros((), BF))
        scores.append(
            lax.dot_general(wide, kbuf[r], (((1,), (1,)), ((), ())), preferred_element_type=F32) * scale
        )
    v_copy.wait()
    fk = fk_ref[...].astype(F32)
    fv = fv_ref[...].astype(F32)
    packed = jnp.zeros((HEADS, HS), F32)
    for r in range(R):
        valid = position < len_ref[r]
        masked = jnp.where(valid, scores[r], -1e30)
        own = jnp.sum(queries[r] * spread(fk[r : r + 1]), axis=1, keepdims=True) * scale
        own = jnp.where(has_own, own, -1e30)
        peak = jnp.maximum(jnp.max(masked, axis=1, keepdims=True), own)
        weight = jnp.where(valid, jnp.exp(masked - peak), 0.0)
        own_weight = jnp.where(has_own, jnp.exp(own - peak), 0.0)
        total = jnp.sum(weight, axis=1, keepdims=True) + own_weight
        high = weight.astype(BF)
        low = (weight - high.astype(F32)).astype(BF)
        both = jnp.dot(jnp.concatenate([high, low], axis=0), vbuf[r], preferred_element_type=F32)
        both = both[:HEADS] + both[HEADS:]
        summed = jnp.concatenate(
            [both[k * GROUP : (k + 1) * GROUP, k * HS : (k + 1) * HS] for k in range(KVH)], axis=0
        )
        summed = summed + own_weight * spread(fv[r : r + 1])
        for i, part in enumerate(split3(peak) + split3(total)):
            packed = jnp.where(lane == i * R + r, part, packed)
        for s in range(S):
            sbuf1[s, r] = summed[s * HD : (s + 1) * HD].astype(BF)
    for s in range(S):
        sbuf1[s, R] = packed[s * HD : (s + 1) * HD].astype(BF)

    logits = logit_ref[...]
    odds = jnp.exp(logits - jnp.max(logits, axis=0, keepdims=True))
    gates = odds / jnp.sum(odds, axis=0, keepdims=True)
    routes = route_ref[...]
    slot_id = lax.broadcasted_iota(jnp.int32, (NL, T), 0)
    place = slot_id % L
    slot_expert = ((slot_id // L) * PIECES) // 2 + place // CAP
    row_id = lax.broadcasted_iota(jnp.int32, (NL, T), 1)
    hits = jnp.zeros((NL, T), F32)
    share = jnp.zeros((NL, T), F32)
    for k in range(routes.shape[0]):
        match = (routes[k : k + 1] == slot_expert) & (row_id // R == exp)
        hits = jnp.where(match, 1.0, hits)
        share = share + jnp.where(match, gates[k : k + 1], 0.0)
    earlier = lax.broadcasted_iota(jnp.int32, (T, T), 0) < lax.broadcasted_iota(jnp.int32, (T, T), 1)
    before = jnp.dot(
        hits.astype(BF), jnp.where(earlier, 1.0, 0.0).astype(BF), preferred_element_type=F32
    )
    taken = (hits > 0.5) & (before == (place % CAP).astype(F32))
    chosen = jnp.where(taken, 1.0, 0.0)
    share = jnp.where(taken, share, 0.0)

    pl.semaphore_wait(barrier, N - 1)

    def copy1(j):
        peer = lax.rem(seq + j, S)
        return pltpu.make_async_remote_copy(
            src_ref=sbuf1.at[peer], dst_ref=rbuf1.at[j], send_sem=ss1.at[j], recv_sem=rs1.at[j],
            device_id={"seq": peer, "expert": exp}, device_id_type=MESH,
        )

    def start1(j, _):
        copy1(j).start()
        return 0

    def wait1(j, _):
        copy1(j).wait_recv()
        return 0

    lax.fori_loop(1, S, start1, 0)
    rbuf1[0] = sbuf1[seq]
    lax.fori_loop(1, S, wait1, 0)

    stats = rbuf1[:, R].astype(F32)
    for r in range(R):
        peak = joined(stats, 0, r)
        total = joined(stats, 3, r)
        factor = jnp.exp(peak - jnp.max(peak, axis=0, keepdims=True))
        att[r] = jnp.sum(factor * rbuf1[:, r].astype(F32), axis=0) / jnp.sum(factor * total, axis=0)
    attended = jnp.concatenate([att[:, h, :] for h in range(HD)], axis=1).astype(BF)

    ow_copy.wait()

    def copy2(j):
        peer = lax.rem(seq + j, S)
        return pltpu.make_async_remote_copy(
            src_ref=sbuf2.at[j], dst_ref=rbuf2.at[j], send_sem=ss2.at[j], recv_sem=rs2.at[j],
            device_id={"seq": peer, "expert": exp}, device_id_type=MESH,
        )

    def project(j):
        cols = pl.ds(pl.multiple_of(lax.rem(seq + j, S) * W, W), W)
        return jnp.dot(attended, owbuf[:, cols], preferred_element_type=F32)

    def start2(j, _):
        sbuf2[j] = project(j).astype(BF)
        copy2(j).start()
        return 0

    def wait2(j, _):
        copy2(j).wait_recv()
        return 0

    lax.fori_loop(1, S, start2, 0)
    own_projected = project(0)
    rbuf2[0] = jnp.zeros((R, W), BF)
    if REUSE:
        pltpu.make_async_copy(wd_hbm.at[NB], owbuf.at[pl.ds(0, FH), :], b_sem.at[NB]).start()
    lax.fori_loop(1, S, wait2, 0)

    own_cols = pl.ds(pl.multiple_of(seq * W, W), W)
    stream = res_ref[:, own_cols].astype(F32) + own_projected + jnp.sum(rbuf2[...].astype(F32), axis=0)
    strm[...] = stream
    squares = jnp.sum(stream * stream, axis=1, keepdims=True)
    parts = split3(squares)
    lane_r = lax.broadcasted_iota(jnp.int32, (R, 128), 1)
    tail = jnp.zeros((R, 128), F32)
    for i in range(3):
        tail = jnp.where(lane_r == i, parts[i], tail)
    sent = jnp.concatenate([stream * gain_ref[:, own_cols], tail], axis=1)
    slots = jnp.dot(
        chosen.astype(BF), jnp.concatenate([sent] * E, axis=0).astype(BF), preferred_element_type=F32
    )
    for t in range(N):
        xsend[t] = slots[t * L : (t + 1) * L].astype(BF)

    def target(j):
        t = lax.rem(me + j, N)
        return t // E, lax.rem(t, E)

    def copy3(j, dst):
        ts, te = target(j)
        return pltpu.make_async_remote_copy(
            src_ref=xsend.at[ts * E + te], dst_ref=dst, send_sem=ss3.at[j], recv_sem=rs3.at[j],
            device_id={"seq": ts, "expert": te}, device_id_type=MESH,
        )

    def start3(j, _):
        copy3(j, xg.at[seq, exp]).start()
        return 0

    def wait3(j, _):
        ts, te = target(N - j)
        copy3(j, xg.at[ts, te]).wait_recv()
        return 0

    lax.fori_loop(1, N, start3, 0)
    xg[seq, exp] = xsend[me]

    lax.fori_loop(1, N, wait3, 0)
    squares = jnp.zeros((M, 1), F32)
    for s in range(S):
        block = jnp.concatenate([xg[s, e].astype(F32) for e in range(E)], axis=0)
        xs[(s * W) // HALF, :, (s * W) % HALF : (s * W) % HALF + W] = block[:, :W].astype(BF)
        squares = squares + jnp.sum(block[:, W:], axis=1, keepdims=True)
    inverse = lax.rsqrt(squares * (1.0 / D) + 1e-6)

    def copy4(c, e):
        return pltpu.make_async_remote_copy(
            src_ref=cbuf.at[c, e], dst_ref=rc.at[me], send_sem=ss4.at[c * E + e], recv_sem=rs4.at[me],
            device_id={"seq": c, "expert": e}, device_id_type=MESH,
        )

    def piece(p, _):
        acts = []
        for half in range(2):
            for m in range(2):
                i = half * 2 + m
                unit = p * 4 + i
                slot = lax.rem(unit, NA)
                a_copy(p, i, slot).wait()
                part = jnp.zeros((M, FH), F32)
                for k in range(0, HALF, HALF):
                    part = part + jnp.dot(
                        xs[half, :, k : k + HALF], abuf[slot, k : k + HALF, :], preferred_element_type=F32
                    )
                if half == 0:
                    acts.append(part)
                else:
                    acts[m] = acts[m] + part
                if TA > NA:

                    @pl.when(unit + NA < TA)
                    def _():
                        a_copy(p + NA // 4, i, slot).start()

        gate_act = acts[0] * inverse
        up_act = acts[1] * inverse
        hidden = (gate_act / (1.0 + jnp.exp(-gate_act)) * up_act).astype(BF)
        local = (lax.broadcasted_iota(jnp.int32, (M, W), 0) % L) // CAP == p // 2
        def combine(view):
            def columns(j, _):
                c = lax.rem(seq + j, S)
                cols = pl.ds(pl.multiple_of(c * W, W), W)
                result = jnp.dot(hidden, view[pl.ds(0, FH), cols], preferred_element_type=F32)
                result = jnp.where(local, result, 0.0)

                @pl.when(p == 0)
                def _():
                    acc[c] = result

                @pl.when(p > 0)
                def _():
                    acc[c] = acc[c] + result

                @pl.when(p == PIECES - 1)
                def _():
                    value = acc[c]
                    for e in range(E):
                        cbuf[c, e] = value[e * L : (e + 1) * L].astype(BF)

                        @pl.when(c * E + e != me)
                        def _():
                            copy4(c, e).start()

                return 0

            lax.fori_loop(1, S + 1, columns, 0)

        slot = lax.rem(p - p // (NB + 1), NB)
        if REUSE:

            @pl.when(p == NB)
            def _():
                pltpu.make_async_copy(wd_hbm.at[p], owbuf.at[pl.ds(0, FH), :], b_sem.at[NB]).wait()
                combine(owbuf)

            @pl.when(p != NB)
            def _():
                b_copy(p, slot).wait()
                combine(bbuf.at[slot])

            @pl.when((p < NB) & (p + NB + 1 < PIECES))
            def _():
                b_copy(p + NB + 1, slot).start()

        else:
            b_copy(p, slot).wait()
            combine(bbuf.at[slot])
        return 0

    lax.fori_loop(0, PIECES, piece, 0)
    rc[me] = cbuf[seq, exp]

    def wait4(j, _):
        ts, te = target(j)
        src = ts * E + te
        pltpu.make_async_remote_copy(
            src_ref=cbuf.at[ts, te], dst_ref=rc.at[src], send_sem=ss4.at[src], recv_sem=rs4.at[src],
            device_id={"seq": ts, "expert": te}, device_id_type=MESH,
        ).wait_recv()
        return 0

    lax.fori_loop(1, N, wait4, 0)
    back = jnp.concatenate([rc[t].astype(F32) for t in range(N)], axis=0).astype(BF)
    share_high = share.astype(BF)
    share_low = (share - share_high.astype(F32)).astype(BF)
    turned = (((0,), (0,)), ((), ()))
    added = lax.dot_general(share_high, back, turned, preferred_element_type=F32)
    added = added + lax.dot_general(share_low, back, turned, preferred_element_type=F32)
    total = strm[...]
    for e in range(E):
        total = total + added[e * R : (e + 1) * R]
    out_ref[...] = total.astype(BF)

    def sent12(j, _):
        copy1(j).wait_send()
        copy2(j).wait_send()
        return 0

    def sent34(j, _):
        copy3(j, xg.at[seq, exp]).wait_send()
        ts, te = target(j)
        copy4(ts, te).wait_send()
        return 0

    lax.fori_loop(1, S, sent12, 0)
    lax.fori_loop(1, N, sent34, 0)


def on_device(
    query, cached_key_block, cached_value_block, fresh_token_key, fresh_token_value, lengths,
    residual_in, o_weight, norm_gain, gate_logits, routes, w_gate, w_up, w_down,
):
    S, E = lax.axis_size("seq"), lax.axis_size("expert")
    R, D = residual_in.shape
    HEADS = query.shape[1] // HEAD_SIZE
    SPAN = cached_key_block.shape[1]
    KV = cached_key_block.shape[2]
    PIECES, _, FH = w_gate.shape
    N, T, W, HD = S * E, E * R, D // S, HEADS // S
    L = max(1, PIECES // 2) * CAP
    M = E * L
    NA, NB = min(UP_SLOTS, PIECES * 4), min(DOWN_SLOTS, PIECES)
    assert PIECES <= 4 and (PIECES <= NB or o_weight.shape[0] >= FH)
    vmem = pl.BlockSpec(memory_space=pltpu.VMEM)
    hbm = pl.BlockSpec(memory_space=pl.ANY)
    dma = pltpu.SemaphoreType.DMA
    read = 2 * (w_gate.size + w_up.size + w_down.size + o_weight.size + 2 * cached_key_block.size)
    return pl.pallas_call(
        functools.partial(layer_kernel, S, E, R, HEADS, D, FH, PIECES, NA, NB),
        out_shape=jax.ShapeDtypeStruct((R, W), BF),
        in_specs=[pl.BlockSpec(memory_space=pltpu.SMEM)] + [vmem] * 7 + [hbm] * 6,
        out_specs=vmem,
        scratch_shapes=[
            pltpu.VMEM((R, SPAN, KV), BF),
            pltpu.VMEM((R, SPAN, KV), BF),
            pltpu.VMEM(o_weight.shape, BF),
            pltpu.VMEM((NA, D // 2, FH), BF),
            pltpu.VMEM((NB, FH, D), BF),
            pltpu.VMEM((HEADS, R, HEAD_SIZE), F32),
            pltpu.VMEM((S, R + 1, HD, HEAD_SIZE), BF),
            pltpu.VMEM((S, R + 1, HD, HEAD_SIZE), BF),
            pltpu.VMEM((R, HD, HEAD_SIZE), F32),
            pltpu.VMEM((S, R, W), BF),
            pltpu.VMEM((S, R, W), BF),
            pltpu.VMEM((R, W), F32),
            pltpu.VMEM((N, L, W + 128), BF),
            pltpu.VMEM((S, E, L, W + 128), BF),
            pltpu.VMEM((2, M, D // 2), BF),
            pltpu.VMEM((S, M, W), F32),
            pltpu.VMEM((S, E, L, W), BF),
            pltpu.VMEM((N, L, W), BF),
            dma((2,)), dma((1,)), dma((NA,)), dma((NB + 1,)),
            dma((S,)), dma((S,)), dma((S,)), dma((S,)),
            dma((N,)), dma((N,)), dma((N,)), dma((N,)),
        ],
        compiler_params=pltpu.CompilerParams(
            collective_id=0, has_side_effects=True, vmem_limit_bytes=63 * 1024 * 1024
        ),
        cost_estimate=pl.CostEstimate(flops=T * read, bytes_accessed=read, transcendentals=0),
    )(
        lengths, query, fresh_token_key, fresh_token_value, residual_in,
        norm_gain.reshape(1, D), gate_logits.T, routes.T,
        cached_key_block, cached_value_block, o_weight, w_gate, w_up, w_down,
    )


def solution(mesh):
    placed = (
        P("expert", None),
        P("expert", "seq", None),
        P("expert", "seq", None),
        P("expert", None),
        P("expert", None),
        P("expert"),
        P("expert", None),
        P("seq", None),
        P(),
        P(),
        P(),
        P(("seq", "expert"), None, None),
        P(("seq", "expert"), None, None),
        P(("seq", "expert"), None, None),
    )
    return jax.shard_map(
        on_device, mesh=mesh, in_specs=placed, out_specs=P("expert", "seq"), check_vma=False
    )
```
